256 devices in a mesh: dp: 16 (over x, y_lo, core), shard: 16 (over z, y_hi).
Axes of the slice: x: 4, y: 4 (y_hi: 2, y_lo: 2; y = y_hi * 2 + y_lo), z: 8, core: 2. Of those that a mesh axis runs over, the one named last changes fastest.
Arguments:
- layer_input: bfloat16 [32768, 8192], P(('dp', 'shard')), may hold values from -6 to 6
- queries: bfloat16 [32768, 4096], P(('dp', 'shard')), may hold values from -200 to 200
- key_rows: bfloat16 [32768, 512], P(('dp', 'shard')), may hold values from -6 to 6
- value_weight: bfloat16 [8192, 512], P('shard'), may hold values from -0.0625 to 0.0625
- segment_ids: int32 [256, 128], P(('dp', 'shard')), may hold values from 0 to 31, never falling along the last dimension, each value on 1 to 64 neighbouring positions
- send_order: int32 [256, 128], P(('dp', 'shard')), may hold values from 0 to 127, each once within a row
- out_grad: bfloat16 [32768, 4096], P(('dp', 'shard')), may hold values from -6 to 6
Outputs:
- attended: bfloat16 [32768, 4096], P(('dp', 'shard'))
- query_grad: bfloat16 [32768, 4096], P(('dp', 'shard'))
- key_grad: bfloat16 [32768, 512], P(('dp', 'shard'))
- input_grad: bfloat16 [32768, 8192], P(('dp', 'shard'))
- weight_grad: float32 [8192, 512], P('shard')
The draws below stay inside these ranges and needn't reach their ends.
Inputs may be any that keep to these rules, and one draw needn't show every extreme that they name: Each device's row of send_order is a permutation of its 128 local rows. `segment_ids`: ids never fall along a device's row; each document has 1 to 64 rows.
All inputs are finite; a program needn't handle non-finite values.
Results may differ from the reference program's by a relative error of at most 0.034.
Values may be sent and summed in bfloat16 or wider, within the bound.
No kernel may reach another device: no remote copies, remote signals or barrier semaphores. Data moves between devices by JAX's collectives and lax.ppermute only.
A program may use at most 128 MiB of HBM per device.

```python
import math
import jax
import jax.numpy as jnp
import numpy as np
from jax import lax

D = 8192
HEADS = 32
KV_HEADS = 4
HD = 128
ROWS = 128
HQW = 4096
KVW = 512
TOKENS = 32768
N_DP = 16
N_SHARD = 16


def draw_queries(key, part):
    key = jax.random.fold_in(key, 7)
    base = jax.random.truncated_normal(key, -5.0, 5.0, (TOKENS, HEADS * HD), jnp.float32)
    return base.astype(jnp.bfloat16)


def block_levels(rng, dims, shards, smallest, top_value):
    gain, own = 1.0, jax.random.fold_in(rng, 6)
    for dim, shards_of in shards:
        draws = jnp.exp(jax.random.uniform(jax.random.fold_in(own, dim), (shards_of,), jnp.float32, smallest / len(shards), top_value / len(shards)))
        gain = gain * jnp.repeat(draws, dims[dim] // shards_of).reshape([-1 if axis == dim else 1 for axis in range(len(dims))])
    return gain


def split_up(count, total, bound, skew):
    portions = [(1 << 20) // math.isqrt(standing ** skew) + 1 for standing in range(2, count + 1)]
    surplus, holding = total - bound - (count - 1), [1] * (count - 1)
    while surplus > 0:
        movable = [i for i in range(count - 1) if holding[i] < bound]
        pool, remaining = sum([portions[i] for i in movable]), surplus
        for i in movable:
            extra = min(bound - holding[i], max(1, remaining * portions[i] // pool), surplus)
            holding[i] = holding[i] + extra
            surplus = surplus - extra
    return np.array([bound] + holding)


def uneven_parts(key, count, total, reach, slope):
    if count == 2:
        one = jax.random.randint(key, (), max(1, total - reach), min(reach, total - 1) + 1)
        return jnp.stack([one, total - one])
    lengths = jnp.asarray(split_up(count, total, reach, slope), jnp.int32)
    twos = (count - 1) // 2
    source_of, receiver = lengths[1:1 + 2 * twos:2], lengths[2:2 + 2 * twos:2]
    room = jnp.minimum(source_of - 1, reach - receiver)
    passed = jax.random.randint(jax.random.fold_in(key, 1), (twos,), 0, 1 << 20) % (room + 1)
    lengths = lengths.at[1:1 + 2 * twos:2].set(source_of - passed).at[2:2 + 2 * twos:2].set(receiver + passed)
    return lengths[jax.random.permutation(jax.random.fold_in(key, 2), count)]


def scatter_about(stream_key, extent, scale, bound, cuts=(), kind=jnp.bfloat16):
    gain = block_levels(stream_key, extent, cuts, -0.22, 0.18) if cuts else 1.0
    entries = jax.random.normal(stream_key, extent, jnp.float32) * scale * gain
    return jnp.minimum(jnp.maximum(entries, -bound), bound).astype(kind)


def setup_inputs(seed: int = 0) -> dict:
    splits = jax.random.split(jax.random.key(seed), 8)
    return {
        "layer_input": scatter_about(splits[0], (TOKENS, D), 1.0, 6.0, ((0, 256),)),
        "queries": draw_queries(jax.random.fold_in(splits[7], 71), 0),
        "key_rows": scatter_about(splits[2], (TOKENS, KVW), 1.0, 6.0, ((0, 256),)),
        "value_weight": scatter_about(splits[3], (D, KVW), D ** -0.5, 0.0625, ((0, 16),)),
        "segment_ids": jax.vmap(lambda own: jnp.searchsorted(jnp.cumsum(uneven_parts(own, ROWS // 4, ROWS, ROWS // 2, 2)), jnp.arange(ROWS), side="right"))(jax.random.split(splits[4], (N_DP * N_SHARD))).reshape((N_DP * N_SHARD, ROWS)).astype(jnp.int32),
        "send_order": jax.vmap(lambda own: jax.random.permutation(own, ROWS))(jax.random.split(splits[5], (N_DP * N_SHARD))).reshape((N_DP * N_SHARD, ROWS)).astype(jnp.int32),
        "out_grad": scatter_about(splits[6], (TOKENS, HQW), 1.0, 6.0, ((0, 256),)),
    }


def migrate(source, send_order):
    width = source.shape[1]
    blocks = source.reshape(N_DP, N_SHARD, ROWS, width)
    picked = jnp.take_along_axis(blocks, send_order.reshape(N_DP, N_SHARD, ROWS, 1), axis=2)
    picked = picked.reshape(N_DP, N_SHARD, N_DP, ROWS // N_DP, width)
    return picked.transpose(2, 1, 0, 3, 4).reshape(-1, width)


def unmigrate(moved, send_order):
    width = moved.shape[1]
    blocks = moved.reshape(N_DP, N_SHARD, N_DP, ROWS // N_DP, width)
    sent = blocks.transpose(2, 1, 0, 3, 4).reshape(N_DP, N_SHARD, ROWS, width)
    inverse = jnp.argsort(send_order.reshape(N_DP, N_SHARD, ROWS), axis=-1).astype(jnp.int32)
    back = jnp.take_along_axis(sent, inverse[..., None], axis=2)
    return back.reshape(-1, width)


def attend(query_rows, key_block, value_block, seg_row, grad_rows):
    count = query_rows.shape[0]
    group_size = HEADS // KV_HEADS
    factor = HD ** -0.5
    query_four = query_rows.reshape(count, KV_HEADS, group_size, HD).astype(jnp.float32)
    key_three = key_block.reshape(count, KV_HEADS, HD).astype(jnp.float32)
    value_three = value_block.reshape(count, KV_HEADS, HD).astype(jnp.float32)
    grad_four = grad_rows.reshape(count, KV_HEADS, group_size, HD).astype(jnp.float32)
    position = jnp.arange(count, dtype=jnp.int32)
    allowed = (seg_row[:, None] == seg_row[None, :]) & (position[None, :] <= position[:, None])
    scores = jnp.einsum("qgrd,kgd->grqk", query_four, key_three) * factor
    scores = jnp.where(allowed, scores, -1e30)
    highest = jnp.max(scores, axis=-1, keepdims=True)
    expon = jnp.exp(scores - highest)
    probs = expon / jnp.sum(expon, axis=-1, keepdims=True)
    probs_b = probs.astype(jnp.bfloat16).astype(jnp.float32)
    attended = jnp.einsum("grqk,kgd->qgrd", probs_b, value_three).astype(jnp.bfloat16)
    dprob = jnp.einsum("qgrd,kgd->grqk", grad_four, value_three)
    delta = jnp.sum(grad_four * attended.astype(jnp.float32), axis=-1)
    delta = jnp.transpose(delta, (1, 2, 0))[..., None]
    dscore = (probs * (dprob - delta)).astype(jnp.bfloat16).astype(jnp.float32)
    query_grad = (jnp.einsum("grqk,kgd->qgrd", dscore, key_three) * factor).astype(jnp.bfloat16)
    key_grad = (jnp.einsum("grqk,qgrd->kgd", dscore, query_four) * factor).astype(jnp.bfloat16)
    value_grad = jnp.einsum("grqk,qgrd->kgd", probs_b, grad_four).astype(jnp.bfloat16)
    return (attended.reshape(count, -1), query_grad.reshape(count, -1),
            key_grad.reshape(count, -1), value_grad.reshape(count, -1))


def reference(layer_input, queries, key_rows, value_weight, segment_ids, send_order, out_grad):
    values = jnp.dot(layer_input, value_weight, preferred_element_type=jnp.float32).astype(jnp.bfloat16)
    moved_q = migrate(queries, send_order)
    moved_k = migrate(key_rows, send_order)
    moved_v = migrate(values, send_order)
    devices = N_DP * N_SHARD

    def one_device(pieces):
        return attend(*pieces)

    attended, query_grad, key_grad, value_grad = lax.map(one_device, (
        moved_q.reshape(devices, ROWS, -1), moved_k.reshape(devices, ROWS, -1),
        moved_v.reshape(devices, ROWS, -1), segment_ids, out_grad.reshape(devices, ROWS, -1)))
    attended = attended.reshape(-1, HEADS * HD)
    query_grad = query_grad.reshape(-1, HEADS * HD)
    key_grad = key_grad.reshape(-1, KV_HEADS * HD)
    value_grad = value_grad.reshape(-1, KV_HEADS * HD)
    input_grad = lax.dot_general(value_grad, value_weight, (((1,), (1,)), ((), ())),
                                 preferred_element_type=jnp.float32).astype(jnp.bfloat16)
    source_grad = unmigrate(value_grad, send_order)
    weight_grad = lax.dot_general(layer_input, source_grad, (((0,), (0,)), ((), ())),
                                  preferred_element_type=jnp.float32)
    return attended, query_grad, key_grad, input_grad, weight_grad
```

```python
import jax
import jax.numpy as jnp
from jax import lax
from jax.experimental import pallas as pl
from jax.experimental.pallas import tpu as pltpu
from jax.sharding import Mesh, PartitionSpec as P

HEADS = 32
KV_HEADS = 4
HD = 128
GROUP = HEADS // KV_HEADS
ROWS = 128
D = 8192
KVW = KV_HEADS * HD
HQW = HEADS * HD
N_DP = 16
N_SHARD = 16
SUB = D // N_DP // N_SHARD
FACTOR = HD ** (-0.5)
VMEM = 60 * 1024 * 1024
LIGHT = pl.CostEstimate(flops=0, bytes_accessed=0, transcendentals=0)

FINE = (("x", 4), ("yl", 2), ("c", 2), ("z", 8), ("yh", 2))
DP = ("x", "yl", "c")
SHARD = ("z", "yh")
ALL = DP + SHARD

NT = (((1,), (1,)), ((), ()))
TN = (((0,), (0,)), ((), ()))


def dot(a, b, dims=(((1,), (0,)), ((), ()))):
    return lax.dot_general(a, b, dims, preferred_element_type=jnp.float32)


def swap(size, offset):
    return [(i, i ^ offset) for i in range(size)]


def sort_matrix(order_row):
    local = lax.broadcasted_iota(jnp.int32, (ROWS, ROWS), 0)
    return (local == jnp.broadcast_to(order_row, (ROWS, ROWS))).astype(jnp.bfloat16)


def sort_qk_kernel(order_ref, q_ref, k_ref, out_ref):
    pick = sort_matrix(order_ref[...])
    out_ref[:, :HQW] = dot(pick, q_ref[...], TN).astype(jnp.bfloat16)
    out_ref[:, HQW:] = dot(pick, k_ref[...], TN).astype(jnp.bfloat16)


def sort_qk(order, queries, key_rows):
    return pl.pallas_call(
        sort_qk_kernel,
        out_shape=jax.ShapeDtypeStruct((ROWS, HQW + KVW), jnp.bfloat16),
        cost_estimate=LIGHT,
        compiler_params=pltpu.CompilerParams(vmem_limit_bytes=VMEM),
        name="sort_qk",
    )(order, queries, key_rows)


PEERS = 8
RING = 8
DEAL = 4 * HD


def deal_columns(place_ref, order_ref, x_ref, deal_ref, rows_ref, put):
    @pl.when(pl.program_id(0) == 0)
    def _():
        a = lax.broadcasted_iota(jnp.int32, (DEAL, 2 * HD), 0)
        b = lax.broadcasted_iota(jnp.int32, (DEAL, 2 * HD), 1)
        deal_ref[...] = (
            ((a >> 7) == ((b >> 5) & 3))
            & (((a >> 5) & 3) == (b >> 7) * 2 + place_ref[2])
            & ((a & 31) == (b & 31))
        ).astype(jnp.bfloat16)

    rows_ref[...] = dot(sort_matrix(order_ref[...]), x_ref[...], TN).astype(jnp.bfloat16)
    for t in range(4):
        lanes = [slice(s * KVW + t * HD, s * KVW + (t + 1) * HD) for s in range(4)]
        part = jnp.concatenate([rows_ref[:, one] for one in lanes], axis=1)
        dealt = dot(part, deal_ref[...]).astype(jnp.bfloat16)
        for u in range(2):
            put(t * 2 + u, dealt[:, u * HD : (u + 1) * HD])


def sort_own_kernel(place_ref, order_ref, x_ref, *refs):
    *out_refs, deal_ref, rows_ref, dealt_ref = refs
    here = place_ref[0] * 2 + place_ref[1]

    def put(n, block):
        dealt_ref[here ^ n] = block

    deal_columns(place_ref, order_ref, x_ref, deal_ref, rows_ref, put)
    for k in range(PEERS):
        out_refs[k][...] = dealt_ref[k]


def sort_other_kernel(place_ref, order_ref, x_ref, out_ref, deal_ref, rows_ref):
    def put(n, block):
        out_ref[n] = block

    deal_columns(place_ref, order_ref, x_ref, deal_ref, rows_ref, put)


def sort_x(place, order, x, own):
    scratch = [pltpu.VMEM((DEAL, 2 * HD), jnp.bfloat16), pltpu.VMEM((ROWS, 4 * KVW), jnp.bfloat16)]
    if own:
        out_specs = [pl.BlockSpec((ROWS, HD), lambda i: (0, i))] * PEERS
        out_shape = [jax.ShapeDtypeStruct((ROWS, KVW), jnp.bfloat16)] * PEERS
        scratch.append(pltpu.VMEM((PEERS, ROWS, HD), jnp.bfloat16))
    else:
        out_specs = pl.BlockSpec((PEERS, ROWS, HD), lambda i: (0, 1, i))
        out_shape = jax.ShapeDtypeStruct((PEERS, 2 * ROWS, KVW), jnp.bfloat16)
    return pl.pallas_call(
        sort_own_kernel if own else sort_other_kernel,
        grid=(4,),
        in_specs=[
            pl.BlockSpec(memory_space=pltpu.SMEM),
            pl.BlockSpec((1, ROWS), lambda i: (0, 0)),
            pl.BlockSpec((ROWS, 4 * KVW), lambda i: (0, i)),
        ],
        out_specs=out_specs,
        out_shape=out_shape,
        scratch_shapes=scratch,
        cost_estimate=LIGHT,
        compiler_params=pltpu.CompilerParams(vmem_limit_bytes=VMEM),
        name="sort_own" if own else "sort_other",
    )(place, order, x)


def probs_kernel(seg_ref, q_ref, k_ref, grad_ref, _, probs_ref, value_grad_ref, payload_ref):
    seg_query = jnp.broadcast_to(seg_ref[...], (ROWS, ROWS))
    seg_key = seg_query.T
    key_at = lax.broadcasted_iota(jnp.int32, (ROWS, ROWS), 0)
    query_at = lax.broadcasted_iota(jnp.int32, (ROWS, ROWS), 1)
    allowed = (seg_key == seg_query) & (key_at <= query_at)
    bias = jnp.where(allowed, 0.0, -1e30).astype(jnp.float32)
    total = jnp.zeros((ROWS, HD), jnp.float32)
    for r in range(GROUP):
        head = slice(r * HD, (r + 1) * HD)
        scores = dot(k_ref[...], q_ref[:, head], NT) * FACTOR
        scores = jnp.where(allowed, scores, bias)
        highest = jnp.max(scores, axis=0, keepdims=True)
        expon = jnp.exp(scores - highest)
        probs = expon / jnp.sum(expon, axis=0, keepdims=True)
        probs_ref[:, head] = probs
        total += dot(probs.astype(jnp.bfloat16), grad_ref[:, head])
    total = total.astype(jnp.bfloat16)
    value_grad_ref[...] = total
    for n in range(PEERS):
        payload_ref[n] = total


def make_probs(seg, moved, out_grad, payload):
    wide = GROUP * HD
    return pl.pallas_call(
        probs_kernel,
        grid=(KV_HEADS,),
        in_specs=[
            pl.BlockSpec((1, ROWS), lambda i: (0, 0)),
            pl.BlockSpec((ROWS, wide), lambda i: (0, i)),
            pl.BlockSpec((ROWS, HD), lambda i: (0, HEADS + i)),
            pl.BlockSpec((ROWS, wide), lambda i: (0, i)),
            pl.BlockSpec(memory_space=pl.ANY),
        ],
        out_specs=[
            pl.BlockSpec((ROWS, wide), lambda i: (0, i)),
            pl.BlockSpec((ROWS, HD), lambda i: (0, i)),
            pl.BlockSpec((PEERS, ROWS, HD), lambda i: (0, 0, i)),
        ],
        out_shape=[
            jax.ShapeDtypeStruct((ROWS, HQW), jnp.float32),
            jax.ShapeDtypeStruct((ROWS, KVW), jnp.bfloat16),
            jax.ShapeDtypeStruct(payload.shape, payload.dtype),
        ],
        input_output_aliases={4: 2},
        cost_estimate=LIGHT,
        compiler_params=pltpu.CompilerParams(vmem_limit_bytes=VMEM),
        name="probs",
    )(seg, moved, moved, out_grad, payload)


def attend_kernel(probs_ref, q_ref, k_ref, v_ref, share_ref, grad_ref, *refs):
    attended_ref, query_grad_ref, key_grad_ref, weight_grad_ref, wide_ref = refs
    weight_grad_ref[...] = share_ref[...].reshape(weight_grad_ref.shape).astype(jnp.float32)

    @pl.when(pl.program_id(0) == 0)
    def _():
        wide_ref[...] = v_ref[...].astype(jnp.float32)

    each = ROWS // N_DP
    own = pl.ds(pl.multiple_of(pl.program_id(0) * each, each), each)
    value = jnp.concatenate([wide_ref[source, own, :] for source in range(N_DP)], axis=0).astype(jnp.bfloat16)
    total = jnp.zeros((ROWS, HD), jnp.float32)
    for r in range(GROUP):
        head = slice(r * HD, (r + 1) * HD)
        probs = probs_ref[:, head]
        probs_b = probs.astype(jnp.bfloat16)
        attended_ref[:, head] = dot(probs_b, value, TN).astype(jnp.bfloat16)
        dprob = dot(value, grad_ref[:, head], NT)
        delta = jnp.sum(probs_b.astype(jnp.float32) * dprob, axis=0, keepdims=True)
        dscore = (probs * (dprob - delta)).astype(jnp.bfloat16)
        query_grad_ref[:, head] = (dot(dscore, k_ref[...], TN) * FACTOR).astype(jnp.bfloat16)
        total += dot(dscore, q_ref[:, head])
    key_grad_ref[...] = (total * FACTOR).astype(jnp.bfloat16)


def attend(probs, moved, got, out_grad):
    wide = GROUP * HD
    block = pl.BlockSpec((ROWS, wide), lambda i: (0, i))
    narrow = pl.BlockSpec((ROWS, HD), lambda i: (0, i))
    return pl.pallas_call(
        attend_kernel,
        grid=(KV_HEADS,),
        in_specs=[
            block,
            block,
            pl.BlockSpec((ROWS, HD), lambda i: (0, HEADS + i)),
            pl.BlockSpec((N_DP, SUB, HD), lambda i: (0, 0, KVW // HD)),
            pl.BlockSpec((N_DP // KV_HEADS, SUB, KVW), lambda i: (i, 0, 0)),
            block,
        ],
        out_specs=[block, block, narrow, pl.BlockSpec((KVW // KV_HEADS, KVW), lambda i: (i, 0))],
        scratch_shapes=[pltpu.VMEM((N_DP, SUB, HD), jnp.float32)],
        out_shape=[
            jax.ShapeDtypeStruct((ROWS, HQW), jnp.bfloat16),
            jax.ShapeDtypeStruct((ROWS, HQW), jnp.bfloat16),
            jax.ShapeDtypeStruct((ROWS, KVW), jnp.bfloat16),
            jax.ShapeDtypeStruct((KVW, KVW), jnp.float32),
        ],
        cost_estimate=LIGHT,
        compiler_params=pltpu.CompilerParams(vmem_limit_bytes=VMEM),
        name="attend",
    )(probs, moved, moved, got, got, out_grad)


def weight_kernel(place_ref, *refs):
    x_refs, both_ref, other_ref, out_ref, wide_ref, total_ref = refs[:PEERS], *refs[PEERS:]
    core = place_ref[2]
    here = place_ref[0] * 2 + place_ref[1]
    for k in range(PEERS):
        wide_ref[(here ^ k) * 2 + core] = x_refs[k][...].astype(jnp.float32)
        wide_ref[k * 2 + 1 - core] = both_ref[k, ROWS:, :].astype(jnp.float32)
    for step in range(PEERS // 2):
        lhs, rhs = [], []
        for at in (step * 2, step * 2 + 1):
            for co in range(2):
                to = at * 2 + (core ^ co)
                rows = pl.ds(pl.multiple_of(to * 8, 8), 8)
                lhs += [wide_ref[source, rows, :] for source in range(N_DP)]
                rhs.append(other_ref[at] if co else both_ref[at, :ROWS, :])
        part = dot(jnp.concatenate(lhs, axis=0).astype(jnp.bfloat16), jnp.concatenate(rhs, axis=0), TN)
        if step == 0:
            total_ref[...] = part
        elif step < PEERS // 2 - 1:
            total_ref[...] += part
        else:
            out_ref[...] = (total_ref[...] + part).astype(jnp.bfloat16).reshape(out_ref.shape)


def weight_part(place, rows_x, both, other):
    vmem = pl.BlockSpec(memory_space=pltpu.VMEM)
    return pl.pallas_call(
        weight_kernel,
        in_specs=[pl.BlockSpec(memory_space=pltpu.SMEM)] + [vmem] * (PEERS + 2),
        out_specs=vmem,
        out_shape=jax.ShapeDtypeStruct((N_SHARD, SUB, KVW), jnp.bfloat16),
        scratch_shapes=[
            pltpu.VMEM((N_DP, ROWS, KVW), jnp.float32),
            pltpu.VMEM((KVW, KVW), jnp.float32),
        ],
        cost_estimate=LIGHT,
        compiler_params=pltpu.CompilerParams(vmem_limit_bytes=VMEM),
        name="weight_part",
    )(place, *rows_x, both, other)


def column_blocks(place_ref):
    deep = D // RING // 2
    for k in range(RING):
        z = (place_ref[4] + k) & (RING - 1)
        for n in range(2):
            yield k, pl.ds(n * deep, deep), pl.ds(pl.multiple_of((z * 2 + (place_ref[3] ^ n)) * deep, deep), deep)


def values_kernel(place_ref, order_ref, x_ref, *refs):
    own_refs, other_refs, out_ref = refs[:RING], refs[RING : 2 * RING], refs[2 * RING]
    mine = jnp.zeros((ROWS, KVW // 2), jnp.float32)
    theirs = jnp.zeros((ROWS, KVW // 2), jnp.float32)
    for k, rows, at in column_blocks(place_ref):
        x = x_ref[:, at]
        mine += dot(x, own_refs[k][rows, :])
        theirs += dot(x, other_refs[k][rows, :])
    first = place_ref[2] == 0
    values = jnp.concatenate([jnp.where(first, mine, theirs), jnp.where(first, theirs, mine)], axis=1)
    values = values.astype(jnp.bfloat16)
    order = jnp.broadcast_to(order_ref[...], (ROWS, ROWS)).T
    pick = (order == lax.broadcasted_iota(jnp.int32, (ROWS, ROWS), 1)).astype(jnp.float32)
    each = ROWS // N_DP
    spread = jnp.concatenate(
        [pick[g * each : (g + 1) * each] for g in range(N_DP) for _ in range(KV_HEADS)], axis=0
    )
    head_of = (lax.broadcasted_iota(jnp.int32, spread.shape, 0) >> 3) & 3
    total = jnp.zeros((N_DP * KV_HEADS * each, HD), jnp.float32)
    for i in range(KV_HEADS):
        one = jnp.where(head_of == i, spread, 0.0).astype(jnp.bfloat16)
        total += dot(one, values[:, i * HD : (i + 1) * HD])
    out_ref[...] = total.astype(jnp.bfloat16).reshape(out_ref.shape)


def input_grad_kernel(place_ref, grad_ref, *refs):
    own_refs, other_refs, out_ref = refs[:RING], refs[RING : 2 * RING], refs[2 * RING]
    half = KVW // 2
    core = place_ref[2]
    grads = [grad_ref[:, pl.ds(pl.multiple_of(at * half, half), half)] for at in (core, 1 - core)]
    for k, rows, at in column_blocks(place_ref):
        part = dot(grads[0], own_refs[k][rows, :], NT) + dot(grads[1], other_refs[k][rows, :], NT)
        out_ref[:, at] = part.astype(jnp.bfloat16)


def with_weight(kernel, name, out_shape, place, *operands):
    vmem = pl.BlockSpec(memory_space=pltpu.VMEM)
    return pl.pallas_call(
        kernel,
        in_specs=[pl.BlockSpec(memory_space=pltpu.SMEM)] + [vmem] * len(operands),
        out_specs=vmem,
        out_shape=jax.ShapeDtypeStruct(out_shape, jnp.bfloat16),
        cost_estimate=LIGHT,
        compiler_params=pltpu.CompilerParams(vmem_limit_bytes=VMEM),
        name=name,
    )(place, *operands)


def share_kernel(shares_ref, v_ref, out_ref):
    total = shares_ref[0].astype(jnp.float32)
    for s in range(1, N_SHARD):
        total += shares_ref[s].astype(jnp.float32)
    total = total.astype(jnp.bfloat16)
    for g in range(N_DP):
        out_ref[g, :, :KVW] = total
    out_ref[:, :, KVW:] = v_ref[...]


def make_share(shares, sent_v):
    return pl.pallas_call(
        share_kernel,
        out_shape=jax.ShapeDtypeStruct((N_DP, SUB, KVW + HD), jnp.bfloat16),
        cost_estimate=LIGHT,
        compiler_params=pltpu.CompilerParams(vmem_limit_bytes=VMEM),
        name="share",
    )(shares, sent_v)


def per_device(layer_input, queries, key_rows, value_weight, segment_ids, send_order, out_grad):
    core = lax.axis_index("c")
    place = jnp.stack([lax.axis_index(name) for name in ("x", "yl", "c", "yh", "z")]).astype(jnp.int32)
    peers = ("x", "yl")
    right = [(i, (i + 1) % RING) for i in range(RING)]
    left = [(i, (i - 1) % RING) for i in range(RING)]
    half = lax.dynamic_slice(value_weight, (0, core * (KVW // 2)), (value_weight.shape[0], KVW // 2))
    other = lax.ppermute(half, "yh", swap(2, 1))
    other_x = lax.ppermute(layer_input, "c", swap(2, 1))
    other_order = lax.ppermute(send_order, "c", swap(2, 1))
    sent = sort_qk(send_order, queries, key_rows)
    rows_x = list(sort_x(place, send_order, layer_input, True))
    other, other_order, sent, rows_x = lax.optimization_barrier((other, other_order, sent, rows_x))
    moved = lax.all_to_all(
        sent.reshape(N_DP, ROWS // N_DP, HQW + KVW), DP, split_axis=0, concat_axis=0, tiled=True
    ).reshape(ROWS, HQW + KVW)
    weight = jnp.concatenate([half, other], axis=0)
    up, down = [weight], [weight]
    payload = sort_x(place, other_order, other_x, False)
    payload, rows_x[5:] = lax.optimization_barrier((payload, rows_x[5:]))
    rows_x = rows_x[:1] + [lax.ppermute(rows_x[k], peers, swap(PEERS, k)) for k in range(1, PEERS)]
    up.append(lax.ppermute(up[0], "z", right))
    down.append(lax.ppermute(down[0], "z", left))

    early = 3
    moved, rows_x[:early], up[1], down[1] = lax.optimization_barrier((moved, rows_x[:early], up[1], down[1]))
    probs, value_grad, payload = make_probs(segment_ids, moved, out_grad, payload)

    up.append(lax.ppermute(up[1], "z", right))
    down.append(lax.ppermute(down[1], "z", left))
    payload, rows_x = lax.optimization_barrier((payload, rows_x))
    both = lax.all_to_all(payload, peers, split_axis=0, concat_axis=0, tiled=True)
    up.append(lax.ppermute(up[2], "z", right))
    down.append(lax.ppermute(down[2], "z", left))
    both, up[3], down[3] = lax.optimization_barrier((both, up[3], down[3]))
    other_grads = lax.ppermute(both[:, :ROWS], "c", swap(2, 1))
    partial = weight_part(place, rows_x, both, other_grads)
    partial, up[3] = lax.optimization_barrier((partial, up[3]))
    shares = lax.all_to_all(partial, SHARD, split_axis=0, concat_axis=0, tiled=True)

    up.append(lax.ppermute(up[3], "z", right))
    own = down[:4] + up[4:0:-1]
    other = [lax.ppermute(one, "c", swap(2, 1)) for one in own]
    sent_v = with_weight(
        values_kernel, "values", (N_DP, SUB, HD), place, send_order, layer_input, *own, *other
    )
    input_grad = with_weight(
        input_grad_kernel, "input_grad", (ROWS, D), place, value_grad, *own, *other
    )

    got = lax.all_to_all(make_share(shares, sent_v), DP, split_axis=0, concat_axis=0, tiled=True)
    got, input_grad = lax.optimization_barrier((got, input_grad))
    attended, query_grad, key_grad, weight_grad = attend(probs, moved, got, out_grad)
    return attended, query_grad, key_grad, input_grad, weight_grad


def solution(mesh):
    fine = Mesh(mesh.devices.reshape([n for _, n in FINE]), [name for name, _ in FINE])
    rows, shard = P(ALL, None), P(SHARD, None)
    return jax.shard_map(
        per_device,
        mesh=fine,
        in_specs=(rows, rows, rows, shard, rows, rows, rows),
        out_specs=(rows, rows, rows, rows, shard),
        check_vma=False,
    )
```

```python
import jax
import jax.numpy as jnp
from jax import lax
from jax.experimental import pallas as pl
from jax.experimental.pallas import tpu as pltpu
from jax.sharding import Mesh, PartitionSpec as P

HEADS = 32
KV_HEADS = 4
HD = 128
GROUP = HEADS // KV_HEADS
ROWS = 128
D = 8192
KVW = KV_HEADS * HD
HQW = HEADS * HD
N_DP = 16
N_SHARD = 16
SUB = D // N_DP // N_SHARD
FACTOR = HD ** (-0.5)
VMEM = 60 * 1024 * 1024
LIGHT = pl.CostEstimate(flops=0, bytes_accessed=0, transcendentals=0)

FINE = (("x", 4), ("yl", 2), ("c", 2), ("z", 8), ("yh", 2))
DP = ("x", "yl", "c")
SHARD = ("z", "yh")
ALL = DP + SHARD

NT = (((1,), (1,)), ((), ()))
TN = (((0,), (0,)), ((), ()))


def dot(a, b, dims=(((1,), (0,)), ((), ()))):
    return lax.dot_general(a, b, dims, preferred_element_type=jnp.float32)


def swap(size, offset):
    return [(i, i ^ offset) for i in range(size)]


def sort_matrix(order_row):
    local = lax.broadcasted_iota(jnp.int32, (ROWS, ROWS), 0)
    return (local == jnp.broadcast_to(order_row, (ROWS, ROWS))).astype(jnp.bfloat16)


def sort_qk_kernel(order_ref, q_ref, k_ref, out_ref):
    pick = sort_matrix(order_ref[...])
    out_ref[:, :HQW] = dot(pick, q_ref[...], TN).astype(jnp.bfloat16)
    out_ref[:, HQW:] = dot(pick, k_ref[...], TN).astype(jnp.bfloat16)


def sort_qk(order, queries, key_rows):
    return pl.pallas_call(
        sort_qk_kernel,
        out_shape=jax.ShapeDtypeStruct((ROWS, HQW + KVW), jnp.bfloat16),
        cost_estimate=LIGHT,
        compiler_params=pltpu.CompilerParams(vmem_limit_bytes=VMEM),
        name="sort_qk",
    )(order, queries, key_rows)


PEERS = 8
RING = 8
DEAL = 4 * HD


def deal_columns(place_ref, order_ref, x_ref, deal_ref, rows_ref, put):
    @pl.when(pl.program_id(0) == 0)
    def _():
        a = lax.broadcasted_iota(jnp.int32, (DEAL, 2 * HD), 0)
        b = lax.broadcasted_iota(jnp.int32, (DEAL, 2 * HD), 1)
        deal_ref[...] = (
            ((a >> 7) == ((b >> 5) & 3))
            & (((a >> 5) & 3) == (b >> 7) * 2 + place_ref[2])
            & ((a & 31) == (b & 31))
        ).astype(jnp.bfloat16)

    rows_ref[...] = dot(sort_matrix(order_ref[...]), x_ref[...], TN).astype(jnp.bfloat16)
    for t in range(4):
        lanes = [slice(s * KVW + t * HD, s * KVW + (t + 1) * HD) for s in range(4)]
        part = jnp.concatenate([rows_ref[:, one] for one in lanes], axis=1)
        dealt = dot(part, deal_ref[...]).astype(jnp.bfloat16)
        for u in range(2):
            put(t * 2 + u, dealt[:, u * HD : (u + 1) * HD])


def sort_own_kernel(place_ref, order_ref, x_ref, out_ref, deal_ref, rows_ref):
    def put(n, block):
        out_ref[n] = block

    deal_columns(place_ref, order_ref, x_ref, deal_ref, rows_ref, put)


def sort_other_kernel(place_ref, order_ref, x_ref, _, out_ref, deal_ref, rows_ref):
    sort_own_kernel(place_ref, order_ref, x_ref, out_ref, deal_ref, rows_ref)


def sort_x(place, order, x, payload=None):
    own = payload is None
    in_specs = [
        pl.BlockSpec(memory_space=pltpu.SMEM),
        pl.BlockSpec((1, ROWS), lambda i: (0, 0)),
        pl.BlockSpec((ROWS, 4 * KVW), lambda i: (0, i)),
    ]
    operands = [place, order, x]
    if not own:
        in_specs.append(pl.BlockSpec(memory_space=pl.ANY))
        operands.append(payload)
    return pl.pallas_call(
        sort_own_kernel if own else sort_other_kernel,
        grid=(4,),
        in_specs=in_specs,
        out_specs=pl.BlockSpec((PEERS, ROWS, HD), lambda i: (0, 0 if own else 1, i)),
        out_shape=jax.ShapeDtypeStruct((PEERS, ROWS if own else 2 * ROWS, KVW), jnp.bfloat16),
        scratch_shapes=[
            pltpu.VMEM((DEAL, 2 * HD), jnp.bfloat16),
            pltpu.VMEM((ROWS, 4 * KVW), jnp.bfloat16),
        ],
        input_output_aliases={} if own else {3: 0},
        cost_estimate=LIGHT,
        compiler_params=pltpu.CompilerParams(vmem_limit_bytes=VMEM),
        name="sort_own" if own else "sort_other",
    )(*operands)


def stack_heads(ref):
    return jnp.concatenate([ref[:, r * HD : (r + 1) * HD] for r in range(GROUP)], axis=0)


def probs_kernel(seg_ref, q_ref, k_ref, grad_ref, probs_ref, value_grad_ref, payload_ref):
    seg_query = jnp.broadcast_to(seg_ref[...], (ROWS, ROWS))
    seg_key = seg_query.T
    key_at = lax.broadcasted_iota(jnp.int32, (ROWS, ROWS), 0)
    query_at = lax.broadcasted_iota(jnp.int32, (ROWS, ROWS), 1)
    allowed = ((seg_key == seg_query) & (key_at <= query_at)).astype(jnp.float32)
    allowed = jnp.concatenate([allowed] * GROUP, axis=1) > 0
    scores = dot(k_ref[...], stack_heads(q_ref), NT) * FACTOR
    scores = jnp.where(allowed, scores, -1e30)
    expon = jnp.exp(scores - jnp.max(scores, axis=0, keepdims=True))
    probs = expon * (1.0 / jnp.sum(expon, axis=0, keepdims=True))
    probs_ref[...] = probs
    total = dot(probs.astype(jnp.bfloat16), stack_heads(grad_ref)).astype(jnp.bfloat16)
    value_grad_ref[...] = total
    for n in range(PEERS):
        payload_ref[n] = total


def make_probs(seg, moved, out_grad):
    wide = GROUP * HD
    return pl.pallas_call(
        probs_kernel,
        grid=(KV_HEADS,),
        in_specs=[
            pl.BlockSpec((1, ROWS), lambda i: (0, 0)),
            pl.BlockSpec((ROWS, wide), lambda i: (0, i)),
            pl.BlockSpec((ROWS, HD), lambda i: (0, HEADS + i)),
            pl.BlockSpec((ROWS, wide), lambda i: (0, i)),
        ],
        out_specs=[
            pl.BlockSpec((ROWS, wide), lambda i: (0, i)),
            pl.BlockSpec((ROWS, HD), lambda i: (0, i)),
            pl.BlockSpec((PEERS, ROWS, HD), lambda i: (0, 0, i)),
        ],
        out_shape=[
            jax.ShapeDtypeStruct((ROWS, HQW), jnp.float32),
            jax.ShapeDtypeStruct((ROWS, KVW), jnp.bfloat16),
            jax.ShapeDtypeStruct((PEERS, 2 * ROWS, KVW), jnp.bfloat16),
        ],
        cost_estimate=LIGHT,
        compiler_params=pltpu.CompilerParams(vmem_limit_bytes=VMEM),
        name="probs",
    )(seg, moved, moved, out_grad)


def attend_kernel(probs_ref, q_ref, k_ref, v_ref, share_ref, grad_ref, *refs):
    attended_ref, query_grad_ref, key_grad_ref, weight_grad_ref, wide_ref = refs
    weight_grad_ref[...] = share_ref[...].reshape(weight_grad_ref.shape).astype(jnp.float32)

    @pl.when(pl.program_id(0) == 0)
    def _():
        wide_ref[...] = v_ref[...].astype(jnp.float32)

    each = ROWS // N_DP
    own = pl.ds(pl.multiple_of(pl.program_id(0) * each, each), each)
    value = jnp.concatenate([wide_ref[source, own, :] for source in range(N_DP)], axis=0).astype(jnp.bfloat16)
    grads, queries = stack_heads(grad_ref), stack_heads(q_ref)
    probs = probs_ref[...]
    probs_b = probs.astype(jnp.bfloat16)
    attended = dot(probs_b, value, TN).astype(jnp.bfloat16)
    dprob = dot(value, grads, NT)
    delta = jnp.sum(probs_b.astype(jnp.float32) * dprob, axis=0, keepdims=True)
    dscore = (probs * (dprob - delta)).astype(jnp.bfloat16)
    query_grad = (dot(dscore, k_ref[...], TN) * FACTOR).astype(jnp.bfloat16)
    for r in range(GROUP):
        head = slice(r * HD, (r + 1) * HD)
        attended_ref[:, head] = attended[head]
        query_grad_ref[:, head] = query_grad[head]
    key_grad_ref[...] = (dot(dscore, queries) * FACTOR).astype(jnp.bfloat16)


def attend(probs, moved, got, out_grad):
    wide = GROUP * HD
    block = pl.BlockSpec((ROWS, wide), lambda i: (0, i))
    narrow = pl.BlockSpec((ROWS, HD), lambda i: (0, i))
    return pl.pallas_call(
        attend_kernel,
        grid=(KV_HEADS,),
        in_specs=[
            block,
            block,
            pl.BlockSpec((ROWS, HD), lambda i: (0, HEADS + i)),
            pl.BlockSpec((N_DP, SUB, HD), lambda i: (0, 0, KVW // HD)),
            pl.BlockSpec((N_DP // KV_HEADS, SUB, KVW), lambda i: (i, 0, 0)),
            block,
        ],
        out_specs=[block, block, narrow, pl.BlockSpec((KVW // KV_HEADS, KVW), lambda i: (i, 0))],
        scratch_shapes=[pltpu.VMEM((N_DP, SUB, HD), jnp.float32)],
        out_shape=[
            jax.ShapeDtypeStruct((ROWS, HQW), jnp.bfloat16),
            jax.ShapeDtypeStruct((ROWS, HQW), jnp.bfloat16),
            jax.ShapeDtypeStruct((ROWS, KVW), jnp.bfloat16),
            jax.ShapeDtypeStruct((KVW, KVW), jnp.float32),
        ],
        cost_estimate=LIGHT,
        compiler_params=pltpu.CompilerParams(vmem_limit_bytes=VMEM),
        name="attend",
    )(probs, moved, moved, got, got, out_grad)


def weight_kernel(place_ref, own_ref, both_ref, other_ref, out_ref, wide_ref, total_ref):
    core = place_ref[2]
    for k in range(PEERS):
        wide_ref[k * 2 + core] = own_ref[k].astype(jnp.float32)
        wide_ref[k * 2 + 1 - core] = both_ref[k, ROWS:, :].astype(jnp.float32)
    for step in range(PEERS // 2):
        lhs, rhs = [], []
        for at in (step * 2, step * 2 + 1):
            for co in range(2):
                to = at * 2 + (core ^ co)
                rows = pl.ds(pl.multiple_of(to * 8, 8), 8)
                lhs += [wide_ref[source, rows, :] for source in range(N_DP)]
                rhs.append(other_ref[at] if co else both_ref[at, :ROWS, :])
        part = dot(jnp.concatenate(lhs, axis=0).astype(jnp.bfloat16), jnp.concatenate(rhs, axis=0), TN)
        if step == 0:
            total_ref[...] = part
        elif step < PEERS // 2 - 1:
            total_ref[...] += part
        else:
            out_ref[...] = (total_ref[...] + part).astype(jnp.bfloat16).reshape(out_ref.shape)


def weight_part(place, own, both, other):
    vmem = pl.BlockSpec(memory_space=pltpu.VMEM)
    return pl.pallas_call(
        weight_kernel,
        in_specs=[pl.BlockSpec(memory_space=pltpu.SMEM)] + [vmem] * 3,
        out_specs=vmem,
        out_shape=jax.ShapeDtypeStruct((N_SHARD, SUB, KVW), jnp.bfloat16),
        scratch_shapes=[
            pltpu.VMEM((N_DP, ROWS, KVW), jnp.float32),
            pltpu.VMEM((KVW, KVW), jnp.float32),
        ],
        cost_estimate=LIGHT,
        compiler_params=pltpu.CompilerParams(vmem_limit_bytes=VMEM),
        name="weight_part",
    )(place, own, both, other)


def column_blocks(place_ref):
    deep = D // RING // 2
    for k in range(RING):
        z = (place_ref[4] + k) & (RING - 1)
        for n in range(2):
            yield k, pl.ds(n * deep, deep), pl.ds(pl.multiple_of((z * 2 + (place_ref[3] ^ n)) * deep, deep), deep)


def values_kernel(place_ref, order_ref, x_ref, *refs):
    own_refs, other_refs, out_ref = refs[:RING], refs[RING : 2 * RING], refs[2 * RING]
    mine = jnp.zeros((ROWS, KVW // 2), jnp.float32)
    theirs = jnp.zeros((ROWS, KVW // 2), jnp.float32)
    for k, rows, at in column_blocks(place_ref):
        x = x_ref[:, at]
        mine += dot(x, own_refs[k][rows, :])
        theirs += dot(x, other_refs[k][rows, :])
    first = place_ref[2] == 0
    values = jnp.concatenate([jnp.where(first, mine, theirs), jnp.where(first, theirs, mine)], axis=1)
    values = values.astype(jnp.bfloat16)
    order = jnp.broadcast_to(order_ref[...], (ROWS, ROWS)).T
    pick = (order == lax.broadcasted_iota(jnp.int32, (ROWS, ROWS), 1)).astype(jnp.float32)
    each = ROWS // N_DP
    spread = jnp.concatenate(
        [pick[g * each : (g + 1) * each] for g in range(N_DP) for _ in range(KV_HEADS)], axis=0
    )
    head_of = (lax.broadcasted_iota(jnp.int32, spread.shape, 0) >> 3) & 3
    total = jnp.zeros((N_DP * KV_HEADS * each, HD), jnp.float32)
    for i in range(KV_HEADS):
        one = jnp.where(head_of == i, spread, 0.0).astype(jnp.bfloat16)
        total += dot(one, values[:, i * HD : (i + 1) * HD])
    out_ref[...] = total.astype(jnp.bfloat16).reshape(out_ref.shape)


def input_grad_kernel(place_ref, grad_ref, *refs):
    own_refs, other_refs, out_ref = refs[:RING], refs[RING : 2 * RING], refs[2 * RING]
    half = KVW // 2
    core = place_ref[2]
    grads = [grad_ref[:, pl.ds(pl.multiple_of(at * half, half), half)] for at in (core, 1 - core)]
    for k, rows, at in column_blocks(place_ref):
        part = dot(grads[0], own_refs[k][rows, :], NT) + dot(grads[1], other_refs[k][rows, :], NT)
        out_ref[:, at] = part.astype(jnp.bfloat16)


def with_weight(kernel, name, out_shape, place, *operands):
    vmem = pl.BlockSpec(memory_space=pltpu.VMEM)
    return pl.pallas_call(
        kernel,
        in_specs=[pl.BlockSpec(memory_space=pltpu.SMEM)] + [vmem] * len(operands),
        out_specs=vmem,
        out_shape=jax.ShapeDtypeStruct(out_shape, jnp.bfloat16),
        cost_estimate=LIGHT,
        compiler_params=pltpu.CompilerParams(vmem_limit_bytes=VMEM),
        name=name,
    )(place, *operands)


def share_kernel(shares_ref, v_ref, out_ref):
    total = shares_ref[0].astype(jnp.float32)
    for s in range(1, N_SHARD):
        total += shares_ref[s].astype(jnp.float32)
    total = total.astype(jnp.bfloat16)
    for g in range(N_DP):
        out_ref[g, :, :KVW] = total
    out_ref[:, :, KVW:] = v_ref[...]


def make_share(shares, sent_v):
    return pl.pallas_call(
        share_kernel,
        out_shape=jax.ShapeDtypeStruct((N_DP, SUB, KVW + HD), jnp.bfloat16),
        cost_estimate=LIGHT,
        compiler_params=pltpu.CompilerParams(vmem_limit_bytes=VMEM),
        name="share",
    )(shares, sent_v)


def per_device(layer_input, queries, key_rows, value_weight, segment_ids, send_order, out_grad):
    core = lax.axis_index("c")
    place = jnp.stack([lax.axis_index(name) for name in ("x", "yl", "c", "yh", "z")]).astype(jnp.int32)
    peers = ("x", "yl")
    right = [(i, (i + 1) % RING) for i in range(RING)]
    left = [(i, (i - 1) % RING) for i in range(RING)]
    half = lax.dynamic_slice(value_weight, (0, core * (KVW // 2)), (value_weight.shape[0], KVW // 2))
    other = lax.ppermute(half, "yh", swap(2, 1))
    other_x = lax.ppermute(layer_input, "c", swap(2, 1))
    other_order = lax.ppermute(send_order, "c", swap(2, 1))
    sent = sort_qk(send_order, queries, key_rows)
    own_x = sort_x(place, send_order, layer_input)
    other, other_order, sent = lax.optimization_barrier((other, other_order, sent))
    moved = lax.all_to_all(
        sent.reshape(N_DP, ROWS // N_DP, HQW + KVW), DP, split_axis=0, concat_axis=0, tiled=True
    ).reshape(ROWS, HQW + KVW)
    weight = jnp.concatenate([half, other], axis=0)
    up, down = [weight], [weight]
    up.append(lax.ppermute(up[0], "z", right))
    down.append(lax.ppermute(down[0], "z", left))
    moved, up[1], down[1], own_x = lax.optimization_barrier((moved, up[1], down[1], own_x))
    own_rows = lax.all_to_all(own_x, peers, split_axis=0, concat_axis=0, tiled=True)
    up.append(lax.ppermute(up[1], "z", right))
    down.append(lax.ppermute(down[1], "z", left))
    probs, value_grad, payload = make_probs(segment_ids, moved, out_grad)
    payload = sort_x(place, other_order, other_x, payload)

    payload, own_rows, up, down = lax.optimization_barrier((payload, own_rows, up, down))
    both = lax.all_to_all(payload, peers, split_axis=0, concat_axis=0, tiled=True)
    up.append(lax.ppermute(up[2], "z", right))
    down.append(lax.ppermute(down[2], "z", left))
    up.append(lax.ppermute(up[3], "z", right))
    both, up, down = lax.optimization_barrier((both, up, down))
    other_grads = lax.ppermute(both[:, :ROWS], "c", swap(2, 1))
    partial = weight_part(place, own_rows, both, other_grads)
    partial, up, down = lax.optimization_barrier((partial, up, down))
    shares = lax.all_to_all(partial, SHARD, split_axis=0, concat_axis=0, tiled=True)

    own = down[:4] + up[4:0:-1]
    other = [lax.ppermute(one, "c", swap(2, 1)) for one in own]
    sent_v = with_weight(
        values_kernel, "values", (N_DP, SUB, HD), place, send_order, layer_input, *own, *other
    )
    input_grad = with_weight(
        input_grad_kernel, "input_grad", (ROWS, D), place, value_grad, *own, *other
    )

    got = lax.all_to_all(make_share(shares, sent_v), DP, split_axis=0, concat_axis=0, tiled=True)
    got, input_grad = lax.optimization_barrier((got, input_grad))
    attended, query_grad, key_grad, weight_grad = attend(probs, moved, got, out_grad)
    return attended, query_grad, key_grad, input_grad, weight_grad


def solution(mesh):
    fine = Mesh(mesh.devices.reshape([n for _, n in FINE]), [name for name, _ in FINE])
    rows, shard = P(ALL, None), P(SHARD, None)
    return jax.shard_map(
        per_device,
        mesh=fine,
        in_specs=(rows, rows, rows, shard, rows, rows, rows),
        out_specs=(rows, rows, rows, rows, shard),
        check_vma=False,
    )
```

```python
import jax
import jax.numpy as jnp
from jax import lax
from jax.experimental import pallas as pl
from jax.experimental.pallas import tpu as pltpu
from jax.sharding import Mesh, PartitionSpec as P

HEADS = 32
KV_HEADS = 4
HD = 128
GROUP = HEADS // KV_HEADS
ROWS = 128
D = 8192
KVW = KV_HEADS * HD
HQW = HEADS * HD
N_DP = 16
N_SHARD = 16
SUB = D // N_DP // N_SHARD
FACTOR = HD ** (-0.5)
VMEM = 60 * 1024 * 1024
VMEM_LATE = 65024 * 1024
LIGHT = pl.CostEstimate(flops=0, bytes_accessed=0, transcendentals=0)

FINE = (("x", 4), ("yl", 2), ("c", 2), ("z", 8), ("yh", 2))
DP = ("x", "yl", "c")
SHARD = ("z", "yh")
ALL = DP + SHARD

NT = (((1,), (1,)), ((), ()))
TN = (((0,), (0,)), ((), ()))


def dot(a, b, dims=(((1,), (0,)), ((), ()))):
    return lax.dot_general(a, b, dims, preferred_element_type=jnp.float32)


def swap(size, offset):
    return [(i, i ^ offset) for i in range(size)]


def sort_matrix(order_row):
    local = lax.broadcasted_iota(jnp.int32, (ROWS, ROWS), 0)
    return (local == jnp.broadcast_to(order_row, (ROWS, ROWS))).astype(jnp.bfloat16)


def sort_qk_kernel(order_ref, q_ref, k_ref, out_ref):
    pick = sort_matrix(order_ref[...])
    out_ref[:, :HQW] = dot(pick, q_ref[...], TN).astype(jnp.bfloat16)
    out_ref[:, HQW:] = dot(pick, k_ref[...], TN).astype(jnp.bfloat16)


def sort_qk(order, queries, key_rows):
    return pl.pallas_call(
        sort_qk_kernel,
        out_shape=jax.ShapeDtypeStruct((ROWS, HQW + KVW), jnp.bfloat16),
        cost_estimate=LIGHT,
        compiler_params=pltpu.CompilerParams(vmem_limit_bytes=VMEM),
        name="sort_qk",
    )(order, queries, key_rows)


PEERS = 8
RING = 8
DEAL = 4 * HD


def deal_columns(place_ref, order_ref, x_ref, deal_ref, rows_ref, put):
    @pl.when(pl.program_id(0) == 0)
    def _():
        a = lax.broadcasted_iota(jnp.int32, (DEAL, 2 * HD), 0)
        b = lax.broadcasted_iota(jnp.int32, (DEAL, 2 * HD), 1)
        deal_ref[...] = (
            ((a >> 7) == ((b >> 5) & 3))
            & (((a >> 5) & 3) == (b >> 7) * 2 + place_ref[2])
            & ((a & 31) == (b & 31))
        ).astype(jnp.bfloat16)

    rows_ref[...] = dot(sort_matrix(order_ref[...]), x_ref[...], TN).astype(jnp.bfloat16)
    for t in range(4):
        lanes = [slice(s * KVW + t * HD, s * KVW + (t + 1) * HD) for s in range(4)]
        part = jnp.concatenate([rows_ref[:, one] for one in lanes], axis=1)
        dealt = dot(part, deal_ref[...]).astype(jnp.bfloat16)
        for u in range(2):
            put(t * 2 + u, dealt[:, u * HD : (u + 1) * HD])


def sort_own_kernel(place_ref, order_ref, x_ref, out_ref, deal_ref, rows_ref):
    def put(n, block):
        out_ref[n] = block

    deal_columns(place_ref, order_ref, x_ref, deal_ref, rows_ref, put)


def sort_other_kernel(place_ref, order_ref, x_ref, _, out_ref, deal_ref, rows_ref):
    sort_own_kernel(place_ref, order_ref, x_ref, out_ref, deal_ref, rows_ref)


def sort_x(place, order, x, payload=None):
    own = payload is None
    in_specs = [
        pl.BlockSpec(memory_space=pltpu.SMEM),
        pl.BlockSpec((1, ROWS), lambda i: (0, 0)),
        pl.BlockSpec((ROWS, 4 * KVW), lambda i: (0, i)),
    ]
    operands = [place, order, x]
    if not own:
        in_specs.append(pl.BlockSpec(memory_space=pl.ANY))
        operands.append(payload)
    return pl.pallas_call(
        sort_own_kernel if own else sort_other_kernel,
        grid=(4,),
        in_specs=in_specs,
        out_specs=pl.BlockSpec((PEERS, ROWS, HD), lambda i: (0, 0 if own else 1, i)),
        out_shape=jax.ShapeDtypeStruct((PEERS, ROWS if own else 2 * ROWS, KVW), jnp.bfloat16),
        scratch_shapes=[
            pltpu.VMEM((DEAL, 2 * HD), jnp.bfloat16),
            pltpu.VMEM((ROWS, 4 * KVW), jnp.bfloat16),
        ],
        input_output_aliases={} if own else {3: 0},
        cost_estimate=LIGHT,
        compiler_params=pltpu.CompilerParams(vmem_limit_bytes=VMEM),
        name="sort_own" if own else "sort_other",
    )(*operands)


def stack_heads(ref):
    return jnp.concatenate([ref[:, r * HD : (r + 1) * HD] for r in range(GROUP)], axis=0)


def probs_kernel(seg_ref, q_ref, k_ref, grad_ref, probs_ref, value_grad_ref, payload_ref):
    seg_query = jnp.broadcast_to(seg_ref[...], (ROWS, ROWS))
    seg_key = seg_query.T
    key_at = lax.broadcasted_iota(jnp.int32, (ROWS, ROWS), 0)
    query_at = lax.broadcasted_iota(jnp.int32, (ROWS, ROWS), 1)
    allowed = ((seg_key == seg_query) & (key_at <= query_at)).astype(jnp.float32)
    allowed = jnp.concatenate([allowed] * GROUP, axis=1) > 0
    scores = dot(k_ref[...], stack_heads(q_ref), NT) * FACTOR
    scores = jnp.where(allowed, scores, -1e30)
    expon = jnp.exp(scores - jnp.max(scores, axis=0, keepdims=True))
    probs = expon * (1.0 / jnp.sum(expon, axis=0, keepdims=True))
    probs_ref[...] = probs
    total = dot(probs.astype(jnp.bfloat16), stack_heads(grad_ref)).astype(jnp.bfloat16)
    value_grad_ref[...] = total
    for n in range(PEERS):
        payload_ref[n] = total


def make_probs(seg, moved, out_grad):
    wide = GROUP * HD
    return pl.pallas_call(
        probs_kernel,
        grid=(KV_HEADS,),
        in_specs=[
            pl.BlockSpec((1, ROWS), lambda i: (0, 0)),
            pl.BlockSpec((ROWS, wide), lambda i: (0, i)),
            pl.BlockSpec((ROWS, HD), lambda i: (0, HEADS + i)),
            pl.BlockSpec((ROWS, wide), lambda i: (0, i)),
        ],
        out_specs=[
            pl.BlockSpec((ROWS, wide), lambda i: (0, i)),
            pl.BlockSpec((ROWS, HD), lambda i: (0, i)),
            pl.BlockSpec((PEERS, ROWS, HD), lambda i: (0, 0, i)),
        ],
        out_shape=[
            jax.ShapeDtypeStruct((ROWS, HQW), jnp.float32),
            jax.ShapeDtypeStruct((ROWS, KVW), jnp.bfloat16),
            jax.ShapeDtypeStruct((PEERS, 2 * ROWS, KVW), jnp.bfloat16),
        ],
        cost_estimate=LIGHT,
        compiler_params=pltpu.CompilerParams(vmem_limit_bytes=VMEM),
        name="probs",
    )(seg, moved, moved, out_grad)


def attend_kernel(probs_ref, q_ref, k_ref, v_ref, share_ref, grad_ref, *refs):
    attended_ref, query_grad_ref, key_grad_ref, weight_grad_ref, wide_ref = refs
    weight_grad_ref[...] = share_ref[...].reshape(weight_grad_ref.shape).astype(jnp.float32)

    @pl.when(pl.program_id(0) == 0)
    def _():
        wide_ref[...] = v_ref[...].astype(jnp.float32)

    each = ROWS // N_DP
    own = pl.ds(pl.multiple_of(pl.program_id(0) * each, each), each)
    value = jnp.concatenate([wide_ref[source, own, :] for source in range(N_DP)], axis=0).astype(jnp.bfloat16)
    grads, queries = stack_heads(grad_ref), stack_heads(q_ref)
    probs = probs_ref[...]
    probs_b = probs.astype(jnp.bfloat16)
    attended = dot(probs_b, value, TN).astype(jnp.bfloat16)
    dprob = dot(value, grads, NT)
    delta = jnp.sum(probs_b.astype(jnp.float32) * dprob, axis=0, keepdims=True)
    dscore = (probs * (dprob - delta)).astype(jnp.bfloat16)
    query_grad = (dot(dscore, k_ref[...], TN) * FACTOR).astype(jnp.bfloat16)
    for r in range(GROUP):
        head = slice(r * HD, (r + 1) * HD)
        attended_ref[:, head] = attended[head]
        query_grad_ref[:, head] = query_grad[head]
    key_grad_ref[...] = (dot(dscore, queries) * FACTOR).astype(jnp.bfloat16)


def attend(probs, moved, got, out_grad):
    wide = GROUP * HD
    block = pl.BlockSpec((ROWS, wide), lambda i: (0, i))
    narrow = pl.BlockSpec((ROWS, HD), lambda i: (0, i))
    return pl.pallas_call(
        attend_kernel,
        grid=(KV_HEADS,),
        in_specs=[
            block,
            block,
            pl.BlockSpec((ROWS, HD), lambda i: (0, HEADS + i)),
            pl.BlockSpec((N_DP, SUB, HD), lambda i: (0, 0, KVW // HD)),
            pl.BlockSpec((N_DP // KV_HEADS, SUB, KVW), lambda i: (i, 0, 0)),
            block,
        ],
        out_specs=[block, block, narrow, pl.BlockSpec((KVW // KV_HEADS, KVW), lambda i: (i, 0))],
        scratch_shapes=[pltpu.VMEM((N_DP, SUB, HD), jnp.float32)],
        out_shape=[
            jax.ShapeDtypeStruct((ROWS, HQW), jnp.bfloat16),
            jax.ShapeDtypeStruct((ROWS, HQW), jnp.bfloat16),
            jax.ShapeDtypeStruct((ROWS, KVW), jnp.bfloat16),
            jax.ShapeDtypeStruct((KVW, KVW), jnp.float32),
        ],
        cost_estimate=LIGHT,
        compiler_params=pltpu.CompilerParams(vmem_limit_bytes=VMEM_LATE),
        name="attend",
    )(probs, moved, moved, got, got, out_grad)


def weight_kernel(place_ref, own_ref, both_ref, other_ref, out_ref, wide_ref):
    core = place_ref[2]
    for k in range(PEERS):
        wide_ref[k * 2 + core] = own_ref[k].astype(jnp.float32)
        wide_ref[k * 2 + 1 - core] = both_ref[k, ROWS:, :].astype(jnp.float32)
    lhs, rhs = [], []
    for at in range(PEERS):
        for co in range(2):
            to = at * 2 + (core ^ co)
            rows = pl.ds(pl.multiple_of(to * 8, 8), 8)
            lhs += [wide_ref[source, rows, :] for source in range(N_DP)]
            rhs.append(other_ref[at] if co else both_ref[at, :ROWS, :])
    total = dot(jnp.concatenate(lhs, axis=0).astype(jnp.bfloat16), jnp.concatenate(rhs, axis=0), TN)
    out_ref[...] = total.astype(jnp.bfloat16).reshape(out_ref.shape)


def weight_part(place, own, both, other):
    vmem = pl.BlockSpec(memory_space=pltpu.VMEM)
    return pl.pallas_call(
        weight_kernel,
        in_specs=[pl.BlockSpec(memory_space=pltpu.SMEM)] + [vmem] * 3,
        out_specs=vmem,
        out_shape=jax.ShapeDtypeStruct((N_SHARD, SUB, KVW), jnp.bfloat16),
        scratch_shapes=[
            pltpu.VMEM((N_DP, ROWS, KVW), jnp.float32),
        ],
        cost_estimate=LIGHT,
        compiler_params=pltpu.CompilerParams(vmem_limit_bytes=VMEM),
        name="weight_part",
    )(place, own, both, other)


def column_blocks(place_ref):
    deep = D // RING // 2
    for k in range(RING):
        z = (place_ref[4] + k) & (RING - 1)
        for n in range(2):
            yield k, pl.ds(n * deep, deep), pl.ds(pl.multiple_of((z * 2 + (place_ref[3] ^ n)) * deep, deep), deep)


def values_kernel(place_ref, order_ref, x_ref, *refs):
    own_refs, other_refs, out_ref = refs[:RING], refs[RING : 2 * RING], refs[2 * RING]
    mine = jnp.zeros((ROWS, KVW // 2), jnp.float32)
    theirs = jnp.zeros((ROWS, KVW // 2), jnp.float32)
    for k, rows, at in column_blocks(place_ref):
        x = x_ref[:, at]
        mine += dot(x, own_refs[k][rows, :])
        theirs += dot(x, other_refs[k][rows, :])
    first = place_ref[2] == 0
    values = jnp.concatenate([jnp.where(first, mine, theirs), jnp.where(first, theirs, mine)], axis=1)
    values = values.astype(jnp.bfloat16)
    order = jnp.broadcast_to(order_ref[...], (ROWS, ROWS)).T
    pick = (order == lax.broadcasted_iota(jnp.int32, (ROWS, ROWS), 1)).astype(jnp.float32)
    each = ROWS // N_DP
    spread = jnp.concatenate(
        [pick[g * each : (g + 1) * each] for g in range(N_DP) for _ in range(KV_HEADS)], axis=0
    )
    head_of = (lax.broadcasted_iota(jnp.int32, spread.shape, 0) >> 3) & 3
    total = jnp.zeros((N_DP * KV_HEADS * each, HD), jnp.float32)
    for i in range(KV_HEADS):
        one = jnp.where(head_of == i, spread, 0.0).astype(jnp.bfloat16)
        total += dot(one, values[:, i * HD : (i + 1) * HD])
    out_ref[...] = total.astype(jnp.bfloat16).reshape(out_ref.shape)


def input_grad_kernel(place_ref, grad_ref, *refs):
    own_refs, other_refs, out_ref = refs[:RING], refs[RING : 2 * RING], refs[2 * RING]
    half = KVW // 2
    core = place_ref[2]
    grads = [grad_ref[:, pl.ds(pl.multiple_of(at * half, half), half)] for at in (core, 1 - core)]
    for k, rows, at in column_blocks(place_ref):
        part = dot(grads[0], own_refs[k][rows, :], NT) + dot(grads[1], other_refs[k][rows, :], NT)
        out_ref[:, at] = part.astype(jnp.bfloat16)


def with_weight(kernel, name, out_shape, place, *operands):
    vmem = pl.BlockSpec(memory_space=pltpu.VMEM)
    return pl.pallas_call(
        kernel,
        in_specs=[pl.BlockSpec(memory_space=pltpu.SMEM)] + [vmem] * len(operands),
        out_specs=vmem,
        out_shape=jax.ShapeDtypeStruct(out_shape, jnp.bfloat16),
        cost_estimate=LIGHT,
        compiler_params=pltpu.CompilerParams(vmem_limit_bytes=VMEM_LATE),
        name=name,
    )(place, *operands)


def share_kernel(shares_ref, v_ref, out_ref):
    total = shares_ref[0].astype(jnp.float32)
    for s in range(1, N_SHARD):
        total += shares_ref[s].astype(jnp.float32)
    total = total.astype(jnp.bfloat16)
    for g in range(N_DP):
        out_ref[g, :, :KVW] = total
    out_ref[:, :, KVW:] = v_ref[...]


def make_share(shares, sent_v):
    whole = lambda i: (0, 0, 0)
    return pl.pallas_call(
        share_kernel,
        grid=(1,),
        in_specs=[pl.BlockSpec(shares.shape, whole), pl.BlockSpec(sent_v.shape, whole)],
        out_specs=pl.BlockSpec((N_DP, SUB, KVW + HD), whole),
        out_shape=jax.ShapeDtypeStruct((N_DP, SUB, KVW + HD), jnp.bfloat16),
        cost_estimate=LIGHT,
        compiler_params=pltpu.CompilerParams(vmem_limit_bytes=VMEM_LATE),
        name="share",
    )(shares, sent_v)


def per_device(layer_input, queries, key_rows, value_weight, segment_ids, send_order, out_grad):
    core = lax.axis_index("c")
    place = jnp.stack([lax.axis_index(name) for name in ("x", "yl", "c", "yh", "z")]).astype(jnp.int32)
    peers = ("x", "yl")
    right = [(i, (i + 1) % RING) for i in range(RING)]
    left = [(i, (i - 1) % RING) for i in range(RING)]
    half = lax.dynamic_slice(value_weight, (0, core * (KVW // 2)), (value_weight.shape[0], KVW // 2))
    other = lax.ppermute(half, "yh", swap(2, 1))
    other_x = lax.ppermute(layer_input, "c", swap(2, 1))
    other_order = lax.ppermute(send_order, "c", swap(2, 1))
    sent = sort_qk(send_order, queries, key_rows)
    own_x = sort_x(place, send_order, layer_input)
    other, other_order, sent = lax.optimization_barrier((other, other_order, sent))
    moved = lax.all_to_all(
        sent.reshape(N_DP, ROWS // N_DP, HQW + KVW), DP, split_axis=0, concat_axis=0, tiled=True
    ).reshape(ROWS, HQW + KVW)
    weight = jnp.concatenate([half, other], axis=0)
    up, down = [weight], [weight]
    up.append(lax.ppermute(up[0], "z", right))
    down.append(lax.ppermute(down[0], "z", left))
    moved, up[1], down[1], own_x = lax.optimization_barrier((moved, up[1], down[1], own_x))
    own_rows = lax.all_to_all(own_x, peers, split_axis=0, concat_axis=0, tiled=True)
    up.append(lax.ppermute(up[1], "z", right))
    down.append(lax.ppermute(down[1], "z", left))
    probs, value_grad, payload = make_probs(segment_ids, moved, out_grad)
    payload = sort_x(place, other_order, other_x, payload)

    payload, own_rows, up, down = lax.optimization_barrier((payload, own_rows, up, down))
    both = lax.all_to_all(payload, peers, split_axis=0, concat_axis=0, tiled=True)
    up.append(lax.ppermute(up[2], "z", right))
    down.append(lax.ppermute(down[2], "z", left))
    up.append(lax.ppermute(up[3], "z", right))
    both, up, down = lax.optimization_barrier((both, up, down))
    other_grads = lax.ppermute(both[:, :ROWS], "c", swap(2, 1))
    partial = weight_part(place, own_rows, both, other_grads)
    partial, up, down = lax.optimization_barrier((partial, up, down))
    shares = lax.all_to_all(partial, SHARD, split_axis=0, concat_axis=0, tiled=True)

    own = down[:4] + up[4:0:-1]
    other = [lax.ppermute(one, "c", swap(2, 1)) for one in own]
    sent_v = with_weight(
        values_kernel, "values", (N_DP, SUB, HD), place, send_order, layer_input, *own, *other
    )
    input_grad = with_weight(
        input_grad_kernel, "input_grad", (ROWS, D), place, value_grad, *own, *other
    )

    got = lax.all_to_all(make_share(shares, sent_v), DP, split_axis=0, concat_axis=0, tiled=True)
    got, input_grad = lax.optimization_barrier((got, input_grad))
    attended, query_grad, key_grad, weight_grad = attend(probs, moved, got, out_grad)
    return attended, query_grad, key_grad, input_grad, weight_grad


def solution(mesh):
    fine = Mesh(mesh.devices.reshape([n for _, n in FINE]), [name for name, _ in FINE])
    rows, shard = P(ALL, None), P(SHARD, None)
    return jax.shard_map(
        per_device,
        mesh=fine,
        in_specs=(rows, rows, rows, shard, rows, rows, rows),
        out_specs=(rows, rows, rows, rows, shard),
        check_vma=False,
    )
```
